128 devices in a mesh: gx: 8 (over y, core), gy: 16 (over x, z).
Axes of the slice: x: 4, y: 4, z: 4, core: 2. Of those that a mesh axis runs over, the one named last changes fastest.
Arguments:
- leaf_multipoles: float32 [35, 65536], P(None, ('gx', 'gy')), may hold values from -6 to 6
- leaf_count: int32 [128], P(('gx', 'gy')), may hold values from 256 to 512, as said below
- send_boxes: int32 [128, 128, 64], P(('gx', 'gy')), may hold values from 0 to 511, as said below
- leaf_sources: int32 [128, 189, 512], P(('gx', 'gy')), may hold values from 0 to 8704, as said below
- top_sources: int32 [128, 189, 9], P(('gx', 'gy')), may hold values from 0 to 1025, as said below
- m2l_leaf: float32 [189, 35, 35], replicated, may hold values from -0.078125 to 0.078125
- m2l_top: float32 [189, 35, 35], replicated, may hold values from -0.078125 to 0.078125
- m2m_up: float32 [64, 35, 35], replicated, may hold values from -0.125 to 0.125
- l2l_down: float32 [64, 35, 35], replicated, may hold values from -1 to 1
Outputs:
- leaf_locals: float32 [35, 65536], P(None, ('gx', 'gy'))
The draws below stay inside these ranges and needn't reach their ends.
Inputs may be any that keep to these rules, and one draw needn't show every extreme that they name: `leaf_count`: each device holds 256 to 512 live leaves; both ends are reached. `send_boxes`: every entry names a live leaf of the sending device. `leaf_sources`: entries index the buffer of own 512 slots, then 64 received slots from each device in device order, then the zero column at 8704; own entries name live leaves; dead target slots hold the zero column. `top_sources`: entries are global top box indices of boxes holding live leaves, or 1025 for none.
All inputs are finite; a program needn't handle non-finite values.
Results may differ from the reference program's by a relative error of at most 0.0003.
Values sent between devices are 32-bit elements; how exact they have to be, the bound alone decides.
No kernel may reach another device: no remote copies, remote signals or barrier semaphores. Data moves between devices by JAX's collectives and lax.ppermute only.
A program may use at most 256 MiB of HBM per device.

```python
import jax
import jax.numpy as jnp
from jax import lax

NC = 35
CLASSES = 189
LEAVES = 512
SCAP = 64
WIN = 9
BOXES = 65536
TOPS = 1025
N_GX = 8
N_GY = 16


def counts_of(key):
    devices = N_GX * N_GY
    key = jax.random.fold_in(key, 11)
    first_key, second_key, third_key = jax.random.split(key, 3)
    counts = jax.random.randint(first_key, (devices,), LEAVES // 2, LEAVES + 1)
    full_rank = jax.random.randint(second_key, (), 0, devices)
    half_rank = (full_rank + 1 + jax.random.randint(third_key, (), 0, devices - 1)) % devices
    ranks = jnp.arange(devices)
    counts = jnp.where(ranks == full_rank, LEAVES, counts)
    counts = jnp.where(ranks == half_rank, LEAVES // 2, counts)
    return counts.astype(jnp.int32)


def slots_of(key):
    devices = N_GX * N_GY
    key = jax.random.fold_in(key, 12)
    return SCAP // 2 + jax.random.randint(key, (devices, devices), 0, SCAP // 2 + 1)


def draw_leaf_count(key, part):
    return counts_of(key)


def draw_send_boxes(key, part):
    devices = N_GX * N_GY
    counts = counts_of(key)
    key = jax.random.fold_in(key, 3)
    upper = jnp.broadcast_to(counts[:, None, None], (devices, devices, SCAP))
    return jax.random.randint(key, (devices, devices, SCAP), 0, upper).astype(jnp.int32)


def draw_leaf_sources(key, part):
    devices = N_GX * N_GY
    counts = counts_of(key)
    live_slots = slots_of(key)
    key = jax.random.fold_in(key, 4)
    keys = jax.random.split(key, 7)
    shape = (devices, CLASSES, LEAVES)
    kinds = jax.random.randint(keys[0], shape, 0, 3)
    own_pick = jax.random.randint(keys[1], shape, 0, jnp.broadcast_to(counts[:, None, None], shape))
    reach_kind = jax.random.randint(keys[2], shape, 0, 4)
    near_step = jax.random.randint(keys[3], shape, 1, 3)
    mid_step = jax.random.randint(keys[4], shape, 1, 9)
    signs = 2 * jax.random.randint(keys[5], shape, 0, 2) - 1
    steps = jnp.where(reach_kind < 2, near_step, mid_step)
    near_offsets = signs * steps % devices
    far_offsets = jax.random.randint(keys[6], shape, 1, devices)
    offsets = jnp.where(reach_kind == 3, far_offsets, near_offsets)
    offsets = jnp.where(offsets == 0, 1, offsets)
    target = jnp.broadcast_to(jnp.arange(devices)[:, None, None], shape)
    source = (target + offsets) % devices
    available = live_slots[source, target]
    slot_pick = jax.random.randint(jax.random.fold_in(keys[3], 9), shape, 0, available)
    remote = LEAVES + source * SCAP + slot_pick
    padding = LEAVES + devices * SCAP
    values = jnp.where(kinds == 1, own_pick, jnp.where(kinds == 2, remote, padding))
    target_live = jnp.arange(LEAVES)[None, None, :] < counts[:, None, None]
    return jnp.where(target_live, values, padding).astype(jnp.int32)


def draw_top_sources(key, part):
    devices = N_GX * N_GY
    counts = counts_of(key)
    starts = jnp.cumsum(counts) - counts
    filled = (jnp.sum(counts) + 63) // 64
    key = jax.random.fold_in(key, 5)
    first_key, second_key = jax.random.split(key, 2)
    shape = (devices, CLASSES, WIN)
    picks = jax.random.randint(first_key, shape, 0, jnp.broadcast_to(filled, shape))
    kinds = jax.random.randint(second_key, shape, 0, 3)
    last_box = (starts % 64 + counts - 1) // 64
    box_live = jnp.arange(WIN)[None, None, :] <= last_box[:, None, None]
    return jnp.where(box_live & (kinds > 0), picks, TOPS).astype(jnp.int32)


def levels(key, shape, cuts, smallest, high):
    def one(position, blocks):
        steps = jax.random.uniform(jax.random.fold_in(jax.random.fold_in(key, 6), position), (blocks,), jnp.float32, smallest / len(cuts), high / len(cuts))
        return jnp.repeat(jnp.exp(steps), shape[position] // blocks).reshape((-1,) + (1,) * (len(shape) - position - 1))

    gain = one(*cuts[0])
    for cut in cuts[1:]:
        gain = gain * one(*cut)
    return gain


def scatter_about(own_key, extent, width, most, pieces=(), held_as=jnp.bfloat16):
    entries = width * jax.random.normal(own_key, extent, jnp.float32)
    if pieces:
        entries = entries * levels(own_key, extent, pieces, -0.22, 0.18)
    return jnp.clip(entries, -most, most).astype(held_as)


def setup_inputs(seed: int = 0) -> dict:
    streams_of = jax.random.split(jax.random.key(seed), 10)
    return {
        "leaf_multipoles": scatter_about(streams_of[0], (NC, BOXES), 1.0, 6.0, ((1, 128),), jnp.float32),
        "leaf_count": draw_leaf_count(jax.random.fold_in(streams_of[9], 71), 0),
        "send_boxes": draw_send_boxes(jax.random.fold_in(streams_of[9], 71), 0),
        "leaf_sources": draw_leaf_sources(jax.random.fold_in(streams_of[9], 71), 0),
        "top_sources": draw_top_sources(jax.random.fold_in(streams_of[9], 71), 0),
        "m2l_leaf": scatter_about(streams_of[5], (CLASSES, NC, NC), (NC * CLASSES) ** -0.5, 0.078125, (), jnp.float32),
        "m2l_top": scatter_about(streams_of[6], (CLASSES, NC, NC), (NC * CLASSES) ** -0.5, 0.078125, (), jnp.float32),
        "m2m_up": scatter_about(streams_of[7], (64, NC, NC), (NC * 64) ** -0.5, 0.125, (), jnp.float32),
        "l2l_down": scatter_about(streams_of[8], (64, NC, NC), NC ** -0.5, 1.0, (), jnp.float32),
    }


highest = lax.Precision.HIGHEST
class_block = 27


def window_moments(moments, first_leaf, m2m_up):
    shift_in = (first_leaf % 64).astype(jnp.int32)
    placed = lax.dynamic_update_slice(jnp.zeros((NC, LEAVES + 64), jnp.float32), moments, (jnp.int32(0), shift_in))
    blocks = placed.reshape(NC, WIN, 64)
    return jnp.einsum("qik,kbq->ib", m2m_up, blocks, precision=highest)


def reference(leaf_multipoles, leaf_count, send_boxes, leaf_sources, top_sources, m2l_leaf, m2l_top, m2m_up, l2l_down):
    devices = N_GX * N_GY
    counts = leaf_count.astype(jnp.int32)
    starts = (jnp.cumsum(counts) - counts).astype(jnp.int32)
    slot_index = jnp.arange(LEAVES, dtype=jnp.int32)
    live_mask = slot_index[None, :] < counts[:, None]
    moments = leaf_multipoles.reshape(NC, devices, LEAVES)
    moments = jnp.where(live_mask[None], moments, jnp.float32(0.0))
    per_device = jnp.transpose(moments, (1, 0, 2))
    partials = jax.vmap(window_moments, in_axes=(0, 0, None))(per_device, starts, m2m_up)
    firsts = (starts // 64).astype(jnp.int32)
    columns = (firsts[:, None] + jnp.arange(WIN, dtype=jnp.int32)[None, :]).reshape(-1)
    top_moments = jnp.zeros((NC, TOPS + 1), jnp.float32).at[:, columns].add(
        jnp.transpose(partials, (1, 0, 2)).reshape(NC, devices * WIN))

    def pick_columns(source_moments, picks):
        return jnp.take(source_moments, picks, axis=1)

    def per_device_far(device):
        own = per_device[device]
        outgoing = send_boxes[:, device, :]
        received = jax.vmap(pick_columns, in_axes=(0, 0), out_axes=1)(per_device, outgoing)
        buffer = jnp.concatenate([own, received.reshape(NC, devices * SCAP), jnp.zeros((NC, 1), jnp.float32)], axis=1)
        class_lists = leaf_sources[device]
        far_field = jnp.zeros((NC, LEAVES), jnp.float32)
        for block_index in range(CLASSES // class_block):
            low = block_index * class_block
            picked = jnp.take(buffer, class_lists[low:low + class_block].reshape(-1), axis=1)
            picked = picked.reshape(NC, class_block, LEAVES)
            far_field = far_field + jnp.einsum("cik,kct->it", m2l_leaf[low:low + class_block], picked, precision=highest)
        gathered = jnp.take(top_moments, top_sources[device].reshape(-1), axis=1).reshape(NC, CLASSES, WIN)
        top_local = jnp.einsum("cik,kcb->ib", m2l_top, gathered, precision=highest)
        spread = jnp.einsum("qik,kb->ibq", l2l_down, top_local, precision=highest).reshape(NC, WIN * 64)
        inherited = lax.dynamic_slice_in_dim(spread, (starts[device] % 64).astype(jnp.int32), LEAVES, 1)
        return jnp.where(live_mask[device][None, :], far_field + inherited, jnp.float32(0.0))

    result = lax.map(per_device_far, jnp.arange(devices, dtype=jnp.int32))
    return jnp.transpose(result, (1, 0, 2)).reshape(NC, devices * LEAVES)
```

```python
import jax
import jax.numpy as jnp
from jax import lax
from jax.experimental import pallas as pl
from jax.experimental.pallas import tpu as pltpu
from jax.sharding import PartitionSpec as P

NC = 35
CLASSES = 189
LEAVES = 512
SCAP = 64
DEVICES = 128
WIN = 9
PAD = 40
HIGH = 48
LANES = 128
STEP = 3
STEPS = CLASSES // STEP
ROWS = LEAVES + DEVICES * SCAP + 8
TOP_ROWS = 1040
TOP_STEP = 9
PEERS = 16
MiB = 2**20

highest = lax.Precision.HIGHEST
axes = ("gx", "gy")
smem = pl.BlockSpec(memory_space=pltpu.SMEM)
vmem = pl.BlockSpec(memory_space=pltpu.VMEM)
anywhere = pl.BlockSpec(memory_space=pl.ANY)


def lane_ids(rows=8):
    return lax.broadcasted_iota(jnp.int32, (rows, LANES), 1)


def three_way(a, b, c):
    lane = lane_ids(a.shape[0])
    return jnp.where(lane < PAD, a, jnp.where(lane < 2 * PAD, b, c))


def split(x):
    high = x.astype(jnp.bfloat16).astype(jnp.float32)
    return high, x - high


def gather_rows(table, picks):
    sub = lax.broadcasted_iota(jnp.int32, (8, LANES), 0)
    block = None
    for s, pick in enumerate(picks):
        row = jnp.broadcast_to(table[pl.ds(pick, 1), :], (8, LANES))
        block = row if block is None else jnp.where(sub == s, row, block)
    return block


def dot_nt(a, b):
    return lax.dot_general(a, b, (((1,), (1,)), ((), ())), preferred_element_type=jnp.float32)


def operator_pieces(padded, operator):
    padded[0:NC, 0:NC] = operator
    high, low = split(padded[...])
    both = high + pltpu.roll(high, PAD, 1) + pltpu.roll(low, 2 * PAD, 1)
    return both.astype(jnp.bfloat16)


def pack_kernel(count, boxes, leaves, out, padded, table, first, second, sem):
    slots = (first, second)

    def fetch(step, slot):
        rows = pl.ds(step * PEERS, PEERS)
        return pltpu.make_async_copy(boxes.at[rows], slots[slot], sem.at[slot])

    fetch(0, 0).start()
    fetch(1, 1).start()
    padded[...] = jnp.zeros_like(padded)
    padded[0:NC, :] = leaves[...]
    held = jnp.full((8, LANES), count[0].astype(jnp.float32))
    for block in range(LEAVES // LANES):
        cols = slice(block * LANES, (block + 1) * LANES)
        x = padded[:, cols]
        table[cols, :] = jnp.concatenate([x, x, x, held], axis=0).T

    def work(step, slot):
        fetch(step, slot).wait()
        for peer in range(PEERS):
            for r in range(0, 24, 8):
                a, b, c = (
                    [slots[slot][peer, g * 24 + r + s] for s in range(8)]
                    if g * 24 + r < SCAP
                    else None
                    for g in range(3)
                )
                a, b = gather_rows(table, a), gather_rows(table, b)
                c = jnp.zeros_like(a) if c is None else gather_rows(table, c)
                out[step * PEERS + peer, r : r + 8, :] = three_way(a, b, c)

        @pl.when(step + 2 < DEVICES // PEERS)
        def _():
            fetch(step + 2, slot).start()

    @pl.loop(0, DEVICES // PEERS // 2)
    def _(pair):
        work(2 * pair, 0)
        work(2 * pair + 1, 1)


def pack(leaf_count, boxes, leaves):
    return pl.pallas_call(
        pack_kernel,
        in_specs=[smem, anywhere, vmem],
        out_specs=vmem,
        out_shape=jax.ShapeDtypeStruct((DEVICES, 24, LANES), jnp.float32),
        scratch_shapes=[
            pltpu.VMEM((PAD, LEAVES), jnp.float32),
            pltpu.VMEM((LEAVES, LANES), jnp.float32),
            pltpu.SMEM((PEERS, SCAP), jnp.int32),
            pltpu.SMEM((PEERS, SCAP), jnp.int32),
            pltpu.SemaphoreType.DMA((2,)),
        ],
        compiler_params=pltpu.CompilerParams(vmem_limit_bytes=16 * MiB),
        cost_estimate=pl.CostEstimate(flops=10**6, bytes_accessed=18 * 10**6, transcendentals=0),
        name="pack",
    )(leaf_count, boxes, leaves)


def pieces_kernel(raw, raw_top, operators, top_operators, square, top_square):
    square[...] = jnp.zeros_like(square)
    top_square[...] = jnp.zeros_like(top_square)

    @pl.loop(0, STEPS)
    def _(step):
        for c in range(STEP):
            place = step * STEP + c
            cols = slice(c * LANES, (c + 1) * LANES)
            operators[step, :, cols] = operator_pieces(square, raw[place])
            cols = pl.ds(pl.multiple_of(place * LANES, LANES), LANES)
            top_operators[:, cols] = operator_pieces(top_square, raw_top[place])


def pieces(raw, raw_top):
    return pl.pallas_call(
        pieces_kernel,
        in_specs=[vmem] * 2,
        out_specs=[vmem] * 2,
        out_shape=[
            jax.ShapeDtypeStruct((STEPS, HIGH, STEP * LANES), jnp.bfloat16),
            jax.ShapeDtypeStruct((HIGH, CLASSES * LANES), jnp.bfloat16),
        ],
        scratch_shapes=[pltpu.VMEM((HIGH, LANES), jnp.float32)] * 2,
        compiler_params=pltpu.CompilerParams(vmem_limit_bytes=32 * MiB),
        cost_estimate=pl.CostEstimate(flops=10**6, bytes_accessed=15 * 10**6, transcendentals=0),
        name="pieces",
    )(raw, raw_top)


def far_kernel(lists, received, leaves, operators, out, padded, table, even, odd, one, two, sem):
    slots, picked = (one, two), (even, odd)

    def fetch(step, slot):
        return pltpu.make_async_copy(lists.at[step], slots[slot], sem.at[slot])

    fetch(0, 0).start()
    fetch(1, 1).start()
    out[...] = jnp.zeros_like(out)
    odd[...] = jnp.zeros_like(odd)
    padded[...] = jnp.zeros_like(padded)
    padded[0:NC, :] = leaves[...]
    rest = jnp.zeros((LANES - 3 * PAD, LANES), jnp.float32)
    for block in range(0, LEAVES, LANES):
        high, low = split(padded[:, block : block + LANES])
        table[block : block + LANES, :] = jnp.concatenate([high, low, high, rest], axis=0).T
    table[ROWS - 8 : ROWS, :] = jnp.zeros((8, LANES), jnp.float32)

    @pl.loop(0, DEVICES // 4)
    def _(quarter):
        for part in range(4):
            sender = quarter * 4 + part
            base = LEAVES + sender * SCAP
            for r in range(0, 24, 8):
                high, low = split(received[sender, r : r + 8, :])
                high_up, high_down = pltpu.roll(high, PAD, 1), pltpu.roll(high, LANES - PAD, 1)
                low_up, low_down = pltpu.roll(low, PAD, 1), pltpu.roll(low, LANES - PAD, 1)
                high_two_up = pltpu.roll(high, 2 * PAD, 1)
                at = pl.multiple_of(base + r, 8)
                table[pl.ds(at, 8), :] = three_way(high, low_up, high_two_up)
                table[pl.ds(at + 24, 8), :] = three_way(high_down, low, high_up)
                if r < 16:
                    high_two_down = pltpu.roll(high, LANES - 2 * PAD, 1)
                    table[pl.ds(at + 48, 8), :] = three_way(high_two_down, low_down, high)

    def multiply(step, slot):
        out[...] += dot_nt(operators[step], picked[slot][...])

    def work(step, slot):
        fetch(step, slot).wait()
        for row in range(0, STEP * LEAVES, 16):
            places = [row + s for s in range(16)]
            picks = [slots[slot][p // LANES, p % LANES] for p in places]
            block = [gather_rows(table, picks[0:8]), gather_rows(table, picks[8:16])]
            c, t = row // LEAVES, row % LEAVES
            block = jnp.concatenate(block, axis=0).astype(jnp.bfloat16)
            picked[slot][t : t + 16, c * LANES : (c + 1) * LANES] = block
        multiply(jnp.maximum(step - 1, 0), 1 - slot)

        @pl.when(step + 2 < STEPS)
        def _():
            fetch(step + 2, slot).start()

    @pl.loop(0, STEPS // 2)
    def _(pair):
        work(2 * pair, 0)
        work(2 * pair + 1, 1)

    work(STEPS - 1, 0)
    multiply(STEPS - 1, 0)


def far(lists, received, leaves, operators):
    return pl.pallas_call(
        far_kernel,
        in_specs=[anywhere] + [vmem] * 3,
        out_specs=vmem,
        out_shape=jax.ShapeDtypeStruct((HIGH, LEAVES), jnp.float32),
        scratch_shapes=[
            pltpu.VMEM((PAD, LEAVES), jnp.float32),
            pltpu.VMEM((ROWS, LANES), jnp.float32),
            pltpu.VMEM((LEAVES, STEP * LANES), jnp.bfloat16),
            pltpu.VMEM((LEAVES, STEP * LANES), jnp.bfloat16),
            pltpu.SMEM((STEP * LEAVES // LANES, LANES), jnp.int32),
            pltpu.SMEM((STEP * LEAVES // LANES, LANES), jnp.int32),
            pltpu.SemaphoreType.DMA((2,)),
        ],
        compiler_params=pltpu.CompilerParams(vmem_limit_bytes=40 * MiB),
        cost_estimate=pl.CostEstimate(flops=10**9, bytes_accessed=100 * 10**6, transcendentals=0),
        name="far",
    )(lists, received, leaves, operators)


def top_kernel(starts, lists, windows, operators, out, table, picked):
    table[...] = jnp.zeros_like(table)
    picked[...] = jnp.zeros_like(picked)
    lane = lane_ids()

    @pl.loop(0, DEVICES, unroll=4)
    def _(sender):
        at = starts[sender]
        x = windows[sender]
        last = pltpu.roll(x, LANES - PAD, 1)
        rows, extra = pl.ds(at, 8), pl.ds(at + 8, 1)
        table[rows, :] += jnp.where(lane < PAD, x, 0.0)
        table[extra, :] += jnp.where(lane < PAD, last, 0.0)[0:1]

    for row in range(0, TOP_ROWS, 8):
        high, low = split(table[row : row + 8, :])
        table[row : row + 8, :] = high + pltpu.roll(low, PAD, 1) + pltpu.roll(high, 2 * PAD, 1)

    @pl.loop(0, CLASSES // TOP_STEP)
    def _(step):
        for c in range(TOP_STEP):
            place = step * TOP_STEP + c
            cols = pl.ds(pl.multiple_of(place * LANES, LANES), LANES)
            picked[0:8, cols] = gather_rows(table, [lists[place * WIN + s] for s in range(8)])
            picked[8:9, cols] = table[pl.ds(lists[place * WIN + 8], 1), :]

    out[...] = dot_nt(operators[...], picked[...].astype(jnp.bfloat16))


def top(starts, lists, windows, operators):
    return pl.pallas_call(
        top_kernel,
        in_specs=[smem] * 2 + [vmem] * 2,
        out_specs=vmem,
        out_shape=jax.ShapeDtypeStruct((HIGH, 16), jnp.float32),
        scratch_shapes=[
            pltpu.VMEM((TOP_ROWS, LANES), jnp.float32),
            pltpu.VMEM((16, CLASSES * LANES), jnp.float32),
        ],
        compiler_params=pltpu.CompilerParams(vmem_limit_bytes=24 * MiB),
        cost_estimate=pl.CostEstimate(flops=10**8, bytes_accessed=20 * 10**6, transcendentals=0),
        name="top",
    )(starts, lists, windows, operators)


def exchange(x):
    return lax.all_to_all(x, axes, split_axis=0, concat_axis=0, tiled=True)


def per_device(
    leaf_multipoles,
    leaf_count,
    send_boxes,
    leaf_sources,
    top_sources,
    m2l_leaf,
    m2l_top,
    m2m_up,
    l2l_down,
):
    received = exchange(pack(leaf_count, send_boxes[0], leaf_multipoles))

    operators, top_operators = pieces(m2l_leaf, m2l_top)
    lists = leaf_sources.reshape(STEPS, STEP * LEAVES // LANES, LANES)
    top_lists = top_sources.reshape(-1)
    received, operators, lists, top_lists = lax.optimization_barrier(
        (received, operators, lists, top_lists)
    )

    counts = received[:, 0, 3 * PAD].astype(jnp.int32)
    ids = jnp.arange(DEVICES)
    before = jnp.where(ids[None, :] < ids[:, None], counts[None, :], 0).sum(axis=1)
    first_boxes = before // 64
    first_leaf = jnp.where(ids < lax.axis_index(axes), counts, 0).sum()
    shift_in = first_leaf % 64
    live_mask = jnp.arange(LEAVES) < leaf_count[0]

    moments = jnp.where(live_mask[None, :], leaf_multipoles, jnp.float32(0.0))
    placed = lax.dynamic_update_slice(
        jnp.zeros((NC, LEAVES + 64), jnp.float32), moments, (0, shift_in)
    )
    blocks = placed.reshape(NC, WIN, 64)
    window = jnp.einsum("qik,kbq->bi", m2m_up, blocks, precision=highest)
    window = jnp.pad(window, ((0, 0), (0, PAD - NC)))
    last = jnp.pad(window[8:9], ((0, 7), (0, LANES - 2 * PAD)))
    own_window = jnp.concatenate([window[0:8], last], axis=1)
    windows = exchange(jnp.broadcast_to(own_window[None], (DEVICES, 8, LANES)))

    far_field = far(lists, received, leaf_multipoles, operators)
    windows, far_field = lax.optimization_barrier((windows, far_field))
    top_local = top(first_boxes, top_lists, windows, top_operators)
    spread = jnp.einsum(
        "qik,kb->ibq", l2l_down, top_local[:NC, :WIN], precision=highest
    ).reshape(NC, WIN * 64)
    inherited = lax.dynamic_slice_in_dim(spread, shift_in, LEAVES, 1)
    return jnp.where(live_mask[None, :], far_field[:NC] + inherited, jnp.float32(0.0))


def solution(mesh):
    in_specs = (
        P(None, axes),
        P(axes),
        P(axes, None, None),
        P(axes, None, None),
        P(axes, None, None),
        P(),
        P(),
        P(),
        P(),
    )
    return jax.shard_map(
        per_device, mesh=mesh, in_specs=in_specs, out_specs=P(None, axes), check_vma=False
    )
```

```python
import jax
import jax.numpy as jnp
from jax import lax
from jax.experimental import pallas as pl
from jax.experimental.pallas import tpu as pltpu
from jax.sharding import PartitionSpec as P

NC = 35
CLASSES = 189
LEAVES = 512
SCAP = 64
DEVICES = 128
WIN = 9
PAD = 40
HIGH = 48
LANES = 128
STEP = 7
STEPS = CLASSES // STEP
ROWS = LEAVES + DEVICES * SCAP + 8
TOP_ROWS = 1040
TOP_STEP = 9
PEERS = 16
SENDERS = 16
MiB = 2**20

highest = lax.Precision.HIGHEST
axes = ("gx", "gy")
smem = pl.BlockSpec(memory_space=pltpu.SMEM)
vmem = pl.BlockSpec(memory_space=pltpu.VMEM)
anywhere = pl.BlockSpec(memory_space=pl.ANY)


def lane_ids(rows=8):
    return lax.broadcasted_iota(jnp.int32, (rows, LANES), 1)


def three_way(a, b, c):
    lane = lane_ids(a.shape[0])
    return jnp.where(lane < PAD, a, jnp.where(lane < 2 * PAD, b, c))


def split(x):
    high = x.astype(jnp.bfloat16).astype(jnp.float32)
    return high, x - high


def gather_rows(table, picks):
    sub = lax.broadcasted_iota(jnp.int32, (8, LANES), 0)
    block = None
    for s, pick in enumerate(picks):
        row = jnp.broadcast_to(table[pl.ds(pick, 1), :], (8, LANES))
        block = row if block is None else jnp.where(sub == s, row, block)
    return block


def dot_nt(a, b):
    return lax.dot_general(a, b, (((1,), (1,)), ((), ())), preferred_element_type=jnp.float32)


def operator_pieces(padded, operator):
    padded[0:NC, 0:NC] = operator
    high, low = split(padded[...])
    both = high + pltpu.roll(high, PAD, 1) + pltpu.roll(low, 2 * PAD, 1)
    return both.astype(jnp.bfloat16)


def pack_kernel(count, boxes, leaves, out, padded, table, first, second, sem):
    slots = (first, second)

    def fetch(step, slot):
        rows = pl.ds(step * PEERS, PEERS)
        return pltpu.make_async_copy(boxes.at[rows], slots[slot], sem.at[slot])

    fetch(0, 0).start()
    fetch(1, 1).start()
    padded[...] = jnp.zeros_like(padded)
    padded[0:NC, :] = leaves[...]
    held = jnp.full((8, LANES), count[0].astype(jnp.float32))
    for block in range(LEAVES // LANES):
        cols = slice(block * LANES, (block + 1) * LANES)
        x = padded[:, cols]
        table[cols, :] = jnp.concatenate([x, x, x, held], axis=0).T

    def work(step, slot):
        fetch(step, slot).wait()
        for peer in range(PEERS):
            for r in range(0, 24, 8):
                a, b, c = (
                    [slots[slot][peer, g * 24 + r + s] for s in range(8)]
                    if g * 24 + r < SCAP
                    else None
                    for g in range(3)
                )
                a, b = gather_rows(table, a), gather_rows(table, b)
                c = jnp.zeros_like(a) if c is None else gather_rows(table, c)
                out[step * PEERS + peer, r : r + 8, :] = three_way(a, b, c)

        @pl.when(step + 2 < DEVICES // PEERS)
        def _():
            fetch(step + 2, slot).start()

    @pl.loop(0, DEVICES // PEERS // 2)
    def _(pair):
        work(2 * pair, 0)
        work(2 * pair + 1, 1)


def pack(leaf_count, boxes, leaves):
    return pl.pallas_call(
        pack_kernel,
        in_specs=[smem, anywhere, vmem],
        out_specs=vmem,
        out_shape=jax.ShapeDtypeStruct((DEVICES, 24, LANES), jnp.float32),
        scratch_shapes=[
            pltpu.VMEM((PAD, LEAVES), jnp.float32),
            pltpu.VMEM((LEAVES, LANES), jnp.float32),
            pltpu.SMEM((PEERS, SCAP), jnp.int32),
            pltpu.SMEM((PEERS, SCAP), jnp.int32),
            pltpu.SemaphoreType.DMA((2,)),
        ],
        compiler_params=pltpu.CompilerParams(vmem_limit_bytes=8 * MiB),
        cost_estimate=pl.CostEstimate(flops=10**6, bytes_accessed=18 * 10**6, transcendentals=0),
        name="pack",
    )(leaf_count, boxes, leaves)


def pieces_kernel(raw, operators, square):
    square[...] = jnp.zeros_like(square)

    @pl.loop(0, STEPS)
    def _(step):
        for c in range(STEP):
            cols = slice(c * LANES, (c + 1) * LANES)
            operators[step, :, cols] = operator_pieces(square, raw[step * STEP + c])


def pieces(raw):
    return pl.pallas_call(
        pieces_kernel,
        in_specs=[vmem],
        out_specs=vmem,
        out_shape=jax.ShapeDtypeStruct((STEPS, HIGH, STEP * LANES), jnp.bfloat16),
        scratch_shapes=[pltpu.VMEM((HIGH, LANES), jnp.float32)],
        compiler_params=pltpu.CompilerParams(vmem_limit_bytes=12 * MiB),
        cost_estimate=pl.CostEstimate(flops=10**6, bytes_accessed=8 * 10**6, transcendentals=0),
        name="pieces",
    )(raw)


def far_kernel(
    lists, received, leaves, operators, out, padded, table, spread, even, odd, one, two, sem
):
    slots, picked = (one, two), (even, odd)

    def fetch(step, slot):
        return pltpu.make_async_copy(lists.at[step], slots[slot], sem.at[slot])

    fetch(0, 0).start()
    fetch(1, 1).start()
    out[...] = jnp.zeros_like(out)
    odd[...] = jnp.zeros_like(odd)
    padded[...] = jnp.zeros_like(padded)
    padded[0:NC, :] = leaves[...]
    rest = jnp.zeros((LANES - 3 * PAD, LANES), jnp.float32)
    for block in range(0, LEAVES, LANES):
        high, low = split(padded[:, block : block + LANES])
        table[block : block + LANES, :] = jnp.concatenate([high, low, high, rest], axis=0).T
    table[ROWS - 8 : ROWS, :] = jnp.zeros((8, LANES), jnp.float32)

    source = lax.broadcasted_iota(jnp.int32, (2 * LANES, 3 * LANES), 0)
    place = lax.broadcasted_iota(jnp.int32, (2 * LANES, 3 * LANES), 1)
    group, at = place >> 7, place & (LANES - 1)
    wanted = jnp.where(at < PAD, at, jnp.where(at < 2 * PAD, at - PAD + LANES, at - 2 * PAD))
    hit = (source == wanted + group * PAD) & (at < 3 * PAD)
    spread[...] = jnp.where(hit, 1.0, 0.0).astype(jnp.bfloat16)

    @pl.loop(0, DEVICES // SENDERS)
    def _(step):
        at = pl.ds(pl.multiple_of(step * SENDERS, SENDERS), SENDERS)
        high, low = split(received[at].reshape(SENDERS * 24, LANES))
        both = jnp.concatenate([high, low], axis=1).astype(jnp.bfloat16)
        made = jnp.dot(both, spread[...], preferred_element_type=jnp.float32)
        for sender in range(SENDERS):
            base = LEAVES + (step * SENDERS + sender) * SCAP
            for g in range(3):
                count = min(24, SCAP - g * 24)
                block = made[sender * 24 : sender * 24 + count, g * LANES : (g + 1) * LANES]
                table[pl.ds(pl.multiple_of(base + g * 24, 8), count), :] = block

    def multiply(step, slot):
        out[...] += dot_nt(operators[step], picked[slot][...])

    def work(step, slot):
        fetch(step, slot).wait()
        for row in range(0, STEP * LEAVES, 16):
            places = [row + s for s in range(16)]
            picks = [slots[slot][p // LANES, p % LANES] for p in places]
            block = [gather_rows(table, picks[0:8]), gather_rows(table, picks[8:16])]
            c, t = row // LEAVES, row % LEAVES
            block = jnp.concatenate(block, axis=0).astype(jnp.bfloat16)
            picked[slot][t : t + 16, c * LANES : (c + 1) * LANES] = block
        multiply(jnp.maximum(step - 1, 0), 1 - slot)

        @pl.when(step + 2 < STEPS)
        def _():
            fetch(step + 2, slot).start()


    @pl.loop(0, STEPS // 2)
    def _(pair):
        work(2 * pair, 0)
        work(2 * pair + 1, 1)

    work(STEPS - 1, 0)
    multiply(STEPS - 1, 0)


def far(lists, received, leaves, operators):
    return pl.pallas_call(
        far_kernel,
        in_specs=[anywhere] + [vmem] * 3,
        out_specs=vmem,
        out_shape=jax.ShapeDtypeStruct((HIGH, LEAVES), jnp.float32),
        scratch_shapes=[
            pltpu.VMEM((PAD, LEAVES), jnp.float32),
            pltpu.VMEM((ROWS, LANES), jnp.float32),
            pltpu.VMEM((2 * LANES, 3 * LANES), jnp.bfloat16),
            pltpu.VMEM((LEAVES, STEP * LANES), jnp.bfloat16),
            pltpu.VMEM((LEAVES, STEP * LANES), jnp.bfloat16),
            pltpu.SMEM((STEP * LEAVES // LANES, LANES), jnp.int32),
            pltpu.SMEM((STEP * LEAVES // LANES, LANES), jnp.int32),
            pltpu.SemaphoreType.DMA((2,)),
        ],
        compiler_params=pltpu.CompilerParams(vmem_limit_bytes=16 * MiB),
        cost_estimate=pl.CostEstimate(flops=10**9, bytes_accessed=100 * 10**6, transcendentals=0),
        name="far",
    )(lists, received, leaves, operators)


def window_kernel(
    me, count, received, leaves, up, out, starts, shift,
    heads, padded, both, rows, row, sem, row_sem,
):
    head = pltpu.make_async_copy(received.at[:, pl.ds(0, 8), :], heads, sem)
    head.start()
    live = lax.broadcasted_iota(jnp.int32, (NC, LEAVES), 1) < count[0]
    padded[...] = jnp.zeros_like(padded)
    padded[0:NC, 0:LEAVES] = jnp.where(live, leaves[...], 0.0)
    both[...] = jnp.zeros_like(both)
    rows[...] = jnp.zeros_like(rows)
    both[:, 0:NC, 0:64] = up[...]
    both[:, 0:NC, 64:128] = up[...]
    head.wait()

    lane = lane_ids(DEVICES)
    sender = lax.broadcasted_iota(jnp.int32, (DEVICES, LANES), 0)
    counts = jnp.where(lane == 3 * PAD, heads[:, 0, :], 0.0)
    large = jnp.floor(counts * 0.0625)
    small = counts - 16.0 * large
    lower = jnp.where(lane < sender, 1.0, 0.0).astype(jnp.bfloat16)

    def sums(x):
        return jnp.dot(lower, x.astype(jnp.bfloat16), preferred_element_type=jnp.float32)

    before = 16.0 * sums(large) + sums(small)
    row[...] = before.T[3 * PAD : 3 * PAD + 8, :].astype(jnp.int32) >> 6
    row_copy = pltpu.make_async_copy(row.at[pl.ds(0, 1), :], starts, row_sem)
    row_copy.start()
    first_leaf = jnp.sum(jnp.where(sender == me[0], before, 0.0)).astype(jnp.int32)
    shift_in = first_leaf & 63
    shift[0] = shift_in
    placed = pltpu.roll(padded[...], shift_in, 1)

    lane = lane_ids(PAD)
    columns = jnp.zeros((PAD, LANES), jnp.float32)
    for t in range(5):
        cols = slice(t * LANES, (t + 1) * LANES)
        for i in range(NC):
            product = both[i, 0:8, :] * placed[0:8, cols]
            for g in range(8, PAD, 8):
                product += both[i, g : g + 8, :] * placed[g : g + 8, cols]
            rows[i : i + 1, :] = jnp.sum(product, axis=0, keepdims=True)
        for half in range(2):
            mine = (lane < 64) if half == 0 else (lane >= 64)
            column = jnp.sum(jnp.where(mine, rows[...], 0.0), axis=1, keepdims=True)
            columns = jnp.where(lane == 2 * t + half, column, columns)
    rest = jnp.zeros((LANES - PAD, LANES), jnp.float32)
    turned = jnp.concatenate([columns, rest], axis=0).T
    last = pltpu.roll(turned[8:16, :], PAD, 1)
    sub = lax.broadcasted_iota(jnp.int32, (8, LANES), 0)
    block = turned[0:8, :] + jnp.where(sub == 0, last, 0.0)
    out[...] = jnp.broadcast_to(block[None], (DEVICES, 8, LANES))
    row_copy.wait()


def window(me, leaf_count, received, leaves, up):
    return pl.pallas_call(
        window_kernel,
        in_specs=[smem, smem, anywhere, vmem, vmem],
        out_specs=[vmem, smem, smem],
        out_shape=[
            jax.ShapeDtypeStruct((DEVICES, 8, LANES), jnp.float32),
            jax.ShapeDtypeStruct((1, DEVICES), jnp.int32),
            jax.ShapeDtypeStruct((1,), jnp.int32),
        ],
        scratch_shapes=[
            pltpu.VMEM((DEVICES, 8, LANES), jnp.float32),
            pltpu.VMEM((PAD, LEAVES + LANES), jnp.float32),
            pltpu.VMEM((NC, PAD, LANES), jnp.float32),
            pltpu.VMEM((PAD, LANES), jnp.float32),
            pltpu.VMEM((8, DEVICES), jnp.int32),
            pltpu.SemaphoreType.DMA,
            pltpu.SemaphoreType.DMA,
        ],
        compiler_params=pltpu.CompilerParams(vmem_limit_bytes=12 * MiB),
        cost_estimate=pl.CostEstimate(flops=10**7, bytes_accessed=3 * 10**6, transcendentals=0),
        name="window",
    )(me, leaf_count, received, leaves, up)


def top_kernel(
    firsts, lists, windows, raw, out, tables, table, picked, turned, square, rows
):
    tables[...] = jnp.zeros_like(tables)
    picked[...] = jnp.zeros_like(picked)
    rows[...] = jnp.zeros_like(rows)
    square[...] = jnp.zeros_like(square)
    lane = lane_ids()
    first_row = lax.broadcasted_iota(jnp.int32, (8, LANES), 0) == 0

    def put(sender, third):
        at = firsts[0, sender]
        x = windows[sender]
        last = pltpu.roll(x, LANES - PAD, 1)
        tables[third, pl.ds(at, 8), :] = jnp.where(lane < PAD, x, 0.0)
        tables[third, pl.ds(at + 8, 8), :] = jnp.where(first_row & (lane < PAD), last, 0.0)

    @pl.loop(0, DEVICES // 3, unroll=2)
    def _(group):
        for third in range(3):
            put(group * 3 + third, third)

    for sender in range(DEVICES // 3 * 3, DEVICES):
        put(sender, sender % 3)
    table[...] = tables[0] + tables[1] + tables[2]

    for b in range(WIN):
        for c in range(0, CLASSES, 8):
            picks = [lists[b, c + s] for s in range(min(8, CLASSES - c))]
            picked[b % 2, c : c + len(picks), :] = gather_rows(table, picks)[: len(picks)]
        for block in range(0, 2 * LANES, LANES):
            turned[b, :, block : block + LANES] = picked[b % 2, block : block + LANES, :].T[0:PAD, :]
    square[:, 0:NC, 0:CLASSES] = raw[...]

    @pl.loop(0, NC, unroll=5)
    def _(i):
        for b in range(WIN):
            product = None
            for g in range(0, PAD, 8):
                for block in range(0, 2 * LANES, LANES):
                    cols = slice(block, block + LANES)
                    term = square[i, g : g + 8, cols] * turned[b, g : g + 8, cols]
                    product = term if product is None else product + term
            rows[b, pl.ds(i, 1), :] = jnp.sum(product, axis=0, keepdims=True)

    lane = lane_ids(PAD)
    columns = jnp.zeros((PAD, LANES), jnp.float32)
    for b in range(WIN):
        columns = jnp.where(lane == b, jnp.sum(rows[b], axis=1, keepdims=True), columns)
    out[...] = columns


def top(firsts, lists, windows, operators):
    return pl.pallas_call(
        top_kernel,
        in_specs=[smem, smem, vmem, vmem],
        out_specs=vmem,
        out_shape=jax.ShapeDtypeStruct((PAD, LANES), jnp.float32),
        scratch_shapes=[
            pltpu.VMEM((3, TOP_ROWS, LANES), jnp.float32),
            pltpu.VMEM((TOP_ROWS, LANES), jnp.float32),
            pltpu.VMEM((2, 2 * LANES, LANES), jnp.float32),
            pltpu.VMEM((WIN, PAD, 2 * LANES), jnp.float32),
            pltpu.VMEM((NC, PAD, 2 * LANES), jnp.float32),
            pltpu.VMEM((WIN, PAD, LANES), jnp.float32),
        ],
        compiler_params=pltpu.CompilerParams(vmem_limit_bytes=12 * MiB),
        cost_estimate=pl.CostEstimate(flops=10**8, bytes_accessed=20 * 10**6, transcendentals=0),
        name="top",
    )(firsts, lists, windows, operators)


def exchange(x):
    return lax.all_to_all(x, axes, split_axis=0, concat_axis=0, tiled=True)


def per_device(
    leaf_multipoles,
    leaf_count,
    send_boxes,
    leaf_sources,
    top_sources,
    m2l_leaf,
    m2l_top,
    m2m_up,
    l2l_down,
):
    received = exchange(pack(leaf_count, send_boxes[0], leaf_multipoles))

    operators = pieces(m2l_leaf)
    lists = leaf_sources.reshape(STEPS, STEP * LEAVES // LANES, LANES)
    top_lists = jnp.transpose(top_sources[0])
    received, operators, lists, top_lists = lax.optimization_barrier(
        (received, operators, lists, top_lists)
    )

    me = lax.axis_index(axes).astype(jnp.int32).reshape(1)
    up = jnp.transpose(m2m_up, (1, 2, 0))
    sent, firsts, shift = window(me, leaf_count, received, leaf_multipoles, up)
    windows = exchange(sent)

    far_field = far(lists, received, leaf_multipoles, operators)
    windows, far_field = lax.optimization_barrier((windows, far_field))
    top_local = top(firsts, top_lists, windows, jnp.transpose(m2l_top, (1, 2, 0)))
    live_mask = jnp.arange(LEAVES) < leaf_count[0]
    spread = jnp.einsum(
        "qik,kb->ibq", l2l_down, top_local[:NC, :WIN], precision=highest
    ).reshape(NC, WIN * 64)
    inherited = lax.dynamic_slice_in_dim(spread, shift[0], LEAVES, 1)
    return jnp.where(live_mask[None, :], far_field[:NC] + inherited, jnp.float32(0.0))


def solution(mesh):
    in_specs = (
        P(None, axes),
        P(axes),
        P(axes, None, None),
        P(axes, None, None),
        P(axes, None, None),
        P(),
        P(),
        P(),
        P(),
    )
    return jax.shard_map(
        per_device, mesh=mesh, in_specs=in_specs, out_specs=P(None, axes), check_vma=False
    )
```

```python
import jax
import jax.numpy as jnp
from jax import lax
from jax.experimental import pallas as pl
from jax.experimental.pallas import tpu as pltpu
from jax.sharding import PartitionSpec as P

NC = 35
CLASSES = 189
LEAVES = 512
SCAP = 64
DEVICES = 128
WIN = 9
PAD = 40
HIGH = 48
LANES = 128
STEP = 7
STEPS = CLASSES // STEP
ROWS = LEAVES + DEVICES * SCAP + 8
TOP_ROWS = 1040
TOP_STEP = 9
PEERS = 16
SENDERS = 16
SENT = 19
THREE = 3 * NC
MiB = 2**20

highest = lax.Precision.HIGHEST
axes = ("gx", "gy")
smem = pl.BlockSpec(memory_space=pltpu.SMEM)
vmem = pl.BlockSpec(memory_space=pltpu.VMEM)
anywhere = pl.BlockSpec(memory_space=pl.ANY)


def lane_ids(rows=8):
    return lax.broadcasted_iota(jnp.int32, (rows, LANES), 1)


def split(x):
    high = x.astype(jnp.bfloat16).astype(jnp.float32)
    return high, x - high


def gather_rows(table, picks):
    sub = lax.broadcasted_iota(jnp.int32, (8, LANES), 0)
    block = None
    for s, pick in enumerate(picks):
        row = jnp.broadcast_to(table[pl.ds(pick, 1), :], (8, LANES))
        block = row if block is None else jnp.where(sub == s, row, block)
    return block


def dot_nt(a, b):
    return lax.dot_general(a, b, (((1,), (1,)), ((), ())), preferred_element_type=jnp.float32)


def operator_pieces(padded, operator):
    padded[0:NC, 0:NC] = operator
    high, low = split(padded[...])
    both = high + pltpu.roll(high, PAD, 1) + pltpu.roll(low, 2 * PAD, 1)
    return both.astype(jnp.bfloat16)


def pack_kernel(count, boxes, leaves, out, stack, table, tail, first, second, sem):
    slots = (first, second)

    def fetch(step, slot):
        rows = pl.ds(step * PEERS, PEERS)
        return pltpu.make_async_copy(boxes.at[rows], slots[slot], sem.at[slot])

    fetch(0, 0).start()
    fetch(1, 1).start()
    for start in range(0, THREE, NC):
        stack[start : start + NC, :] = leaves[...]
    stack[THREE:LANES, :] = leaves[0 : LANES - THREE, :]
    for block in range(0, LEAVES, LANES):
        table[block : block + LANES, :] = stack[:, block : block + LANES].T
    stack[...] = jnp.zeros_like(stack)
    stack[THREE : THREE + NC - 23, :] = leaves[23:NC, :]
    stack[LANES - 8 : LANES, :] = jnp.full((8, LEAVES), count[0].astype(jnp.float32))
    for block in range(0, LEAVES, LANES):
        tail[block : block + LANES, :] = stack[:, block : block + LANES].T
    lane = lane_ids()

    def work(step, slot):
        fetch(step, slot).wait()
        for peer in range(PEERS):
            for r in range(0, SENT, 8):
                size = min(8, SENT - r)
                a, b, c = (
                    gather_rows(table, [slots[slot][peer, g * SENT + r + s] for s in range(size)])
                    for g in range(3)
                )
                block = jnp.where(lane < NC, a, jnp.where(lane < 2 * NC, b, c))
                ends = []
                for row in range(r, min(r + 8, 14)):
                    pick = slots[slot][peer, 3 * SENT + row % 7]
                    ends.append((table if row < 7 else tail)[pl.ds(pick, 1), :])
                if ends:
                    sub = lax.broadcasted_iota(jnp.int32, (8, LANES), 0)
                    end = jnp.broadcast_to(ends[0], (8, LANES))
                    for s in range(1, len(ends)):
                        end = jnp.where(sub == s, jnp.broadcast_to(ends[s], (8, LANES)), end)
                    block = jnp.where(lane < THREE, block, end)
                at = step * (PEERS * SENT) + peer * SENT + r
                out[pl.ds(at, size), :] = block[:size]

        @pl.when(step + 2 < DEVICES // PEERS)
        def _():
            fetch(step + 2, slot).start()

    @pl.loop(0, DEVICES // PEERS // 2)
    def _(pair):
        work(2 * pair, 0)
        work(2 * pair + 1, 1)


def pack(leaf_count, boxes, leaves):
    return pl.pallas_call(
        pack_kernel,
        in_specs=[smem, anywhere, vmem],
        out_specs=vmem,
        out_shape=jax.ShapeDtypeStruct((DEVICES * SENT, LANES), jnp.float32),
        scratch_shapes=[
            pltpu.VMEM((LANES, LEAVES), jnp.float32),
            pltpu.VMEM((LEAVES, LANES), jnp.float32),
            pltpu.VMEM((LEAVES, LANES), jnp.float32),
            pltpu.SMEM((PEERS, SCAP), jnp.int32),
            pltpu.SMEM((PEERS, SCAP), jnp.int32),
            pltpu.SemaphoreType.DMA((2,)),
        ],
        compiler_params=pltpu.CompilerParams(vmem_limit_bytes=8 * MiB),
        cost_estimate=pl.CostEstimate(flops=10**6, bytes_accessed=18 * 10**6, transcendentals=0),
        name="pack",
    )(leaf_count, boxes, leaves)


def pieces_kernel(raw, operators, square):
    square[...] = jnp.zeros_like(square)

    @pl.loop(0, STEPS)
    def _(step):
        for c in range(STEP):
            cols = slice(c * LANES, (c + 1) * LANES)
            operators[step, :, cols] = operator_pieces(square, raw[step * STEP + c])


def pieces(raw):
    return pl.pallas_call(
        pieces_kernel,
        in_specs=[vmem],
        out_specs=vmem,
        out_shape=jax.ShapeDtypeStruct((STEPS, HIGH, STEP * LANES), jnp.bfloat16),
        scratch_shapes=[pltpu.VMEM((HIGH, LANES), jnp.float32)],
        compiler_params=pltpu.CompilerParams(vmem_limit_bytes=12 * MiB),
        cost_estimate=pl.CostEstimate(flops=10**6, bytes_accessed=8 * 10**6, transcendentals=0),
        name="pieces",
    )(raw)


def far_kernel(
    lists, received, leaves, operators, out, padded, table, spread, made, even, odd, one, two, sem
):
    slots, picked = (one, two), (even, odd)

    def fetch(step, slot):
        return pltpu.make_async_copy(lists.at[step], slots[slot], sem.at[slot])

    fetch(0, 0).start()
    fetch(1, 1).start()
    out[...] = jnp.zeros_like(out)
    odd[...] = jnp.zeros_like(odd)
    padded[...] = jnp.zeros_like(padded)
    padded[0:NC, :] = leaves[...]
    rest = jnp.zeros((LANES - 3 * PAD, LANES), jnp.float32)
    for block in range(0, LEAVES, LANES):
        high, low = split(padded[:, block : block + LANES])
        table[block : block + LANES, :] = jnp.concatenate([high, low, high, rest], axis=0).T
    table[ROWS - 8 : ROWS, :] = jnp.zeros((8, LANES), jnp.float32)

    source = lax.broadcasted_iota(jnp.int32, (2 * LANES, 5 * LANES), 0)
    place = lax.broadcasted_iota(jnp.int32, (2 * LANES, 5 * LANES), 1)
    group, at = place >> 7, place & (LANES - 1)
    third = jnp.where(at < PAD, 0, jnp.where(at < 2 * PAD, 1, 2))
    k = at - third * PAD
    wanted = jnp.where(group < 3, group * NC + k, jnp.where(group == 3, THREE + k, THREE - 23 + k))
    wanted = wanted + jnp.where(third == 1, LANES, 0)
    held = (k < NC) & ((group < 3) | ((group == 3) & (k < 23)) | ((group == 4) & (k >= 23)))
    hit = (source == wanted) & held & (at < 3 * PAD)
    spread[...] = jnp.where(hit, 1.0, 0.0).astype(jnp.bfloat16)

    @pl.loop(0, DEVICES // SENDERS)
    def _(step):
        rows = SENDERS * SENT
        x = received[pl.ds(pl.multiple_of(step * rows, 8), rows), :]
        both = jnp.concatenate(split(x), axis=1).astype(jnp.bfloat16)
        made[...] = jnp.dot(both, spread[...], preferred_element_type=jnp.float32)
        for sender in range(SENDERS):
            base = LEAVES + (step * SENDERS + sender) * SCAP
            top_row = sender * SENT
            for g in range(3):
                for r in range(0, SENT, 8):
                    size = min(8, SENT - r)
                    block = made[top_row + r : top_row + r + size, g * LANES : (g + 1) * LANES]
                    table[pl.ds(base + g * SENT + r, size), :] = block
            ends = made[top_row : top_row + 7, 3 * LANES : 4 * LANES]
            ends += made[top_row + 7 : top_row + 14, 4 * LANES : 5 * LANES]
            table[pl.ds(base + 3 * SENT, 7), :] = ends

    def multiply(step, slot):
        out[...] += dot_nt(operators[step], picked[slot][...])

    def work(step, slot):
        fetch(step, slot).wait()
        for row in range(0, STEP * LEAVES, 16):
            places = [row + s for s in range(16)]
            picks = [slots[slot][p // LANES, p % LANES] for p in places]
            block = [gather_rows(table, picks[0:8]), gather_rows(table, picks[8:16])]
            c, t = row // LEAVES, row % LEAVES
            block = jnp.concatenate(block, axis=0).astype(jnp.bfloat16)
            picked[slot][t : t + 16, c * LANES : (c + 1) * LANES] = block
        multiply(jnp.maximum(step - 1, 0), 1 - slot)

        @pl.when(step + 2 < STEPS)
        def _():
            fetch(step + 2, slot).start()


    @pl.loop(0, STEPS // 2)
    def _(pair):
        work(2 * pair, 0)
        work(2 * pair + 1, 1)

    work(STEPS - 1, 0)
    multiply(STEPS - 1, 0)


def far(lists, received, leaves, operators):
    return pl.pallas_call(
        far_kernel,
        in_specs=[anywhere] + [vmem] * 3,
        out_specs=vmem,
        out_shape=jax.ShapeDtypeStruct((HIGH, LEAVES), jnp.float32),
        scratch_shapes=[
            pltpu.VMEM((PAD, LEAVES), jnp.float32),
            pltpu.VMEM((ROWS, LANES), jnp.float32),
            pltpu.VMEM((2 * LANES, 5 * LANES), jnp.bfloat16),
            pltpu.VMEM((SENDERS * SENT, 5 * LANES), jnp.float32),
            pltpu.VMEM((LEAVES, STEP * LANES), jnp.bfloat16),
            pltpu.VMEM((LEAVES, STEP * LANES), jnp.bfloat16),
            pltpu.SMEM((STEP * LEAVES // LANES, LANES), jnp.int32),
            pltpu.SMEM((STEP * LEAVES // LANES, LANES), jnp.int32),
            pltpu.SemaphoreType.DMA((2,)),
        ],
        compiler_params=pltpu.CompilerParams(vmem_limit_bytes=16 * MiB),
        cost_estimate=pl.CostEstimate(flops=10**9, bytes_accessed=100 * 10**6, transcendentals=0),
        name="far",
    )(lists, received, leaves, operators)


def window_kernel(
    me, count, received, leaves, up, out, starts, shift,
    padded, both, rows, row, row_sem,
):
    live = lax.broadcasted_iota(jnp.int32, (NC, LEAVES), 1) < count[0]
    padded[...] = jnp.zeros_like(padded)
    padded[0:NC, 0:LEAVES] = jnp.where(live, leaves[...], 0.0)
    both[...] = jnp.zeros_like(both)
    rows[...] = jnp.zeros_like(rows)
    both[:, 0:NC, 0:64] = up[...]
    both[:, 0:NC, 64:128] = up[...]

    lane = lane_ids(DEVICES)
    sender = lax.broadcasted_iota(jnp.int32, (DEVICES, LANES), 0)
    heads = [[(s + r) * SENT + 7 for r in range(8)] for s in range(0, DEVICES, 8)]
    heads = jnp.concatenate([gather_rows(received, picks) for picks in heads], axis=0)
    counts = jnp.where(lane == LANES - 1, heads, 0.0)
    large = jnp.floor(counts * 0.0625)
    small = counts - 16.0 * large
    lower = jnp.where(lane < sender, 1.0, 0.0).astype(jnp.bfloat16)

    def sums(x):
        return jnp.dot(lower, x.astype(jnp.bfloat16), preferred_element_type=jnp.float32)

    before = 16.0 * sums(large) + sums(small)
    row[...] = before.T[LANES - 8 : LANES, :].astype(jnp.int32) >> 6
    row_copy = pltpu.make_async_copy(row.at[pl.ds(7, 1), :], starts, row_sem)
    row_copy.start()
    first_leaf = jnp.sum(jnp.where(sender == me[0], before, 0.0)).astype(jnp.int32)
    shift_in = first_leaf & 63
    shift[0] = shift_in
    placed = pltpu.roll(padded[...], shift_in, 1)

    lane = lane_ids(PAD)
    columns = jnp.zeros((PAD, LANES), jnp.float32)
    for t in range(5):
        cols = slice(t * LANES, (t + 1) * LANES)
        for i in range(NC):
            product = both[i, 0:8, :] * placed[0:8, cols]
            for g in range(8, PAD, 8):
                product += both[i, g : g + 8, :] * placed[g : g + 8, cols]
            rows[i : i + 1, :] = jnp.sum(product, axis=0, keepdims=True)
        for half in range(2):
            mine = (lane < 64) if half == 0 else (lane >= 64)
            column = jnp.sum(jnp.where(mine, rows[...], 0.0), axis=1, keepdims=True)
            columns = jnp.where(lane == 2 * t + half, column, columns)
    rest = jnp.zeros((LANES - PAD, LANES), jnp.float32)
    turned = jnp.concatenate([columns, rest], axis=0).T
    last = pltpu.roll(turned[8:16, :], PAD, 1)
    sub = lax.broadcasted_iota(jnp.int32, (8, LANES), 0)
    block = turned[0:8, :] + jnp.where(sub == 0, last, 0.0)
    out[...] = jnp.broadcast_to(block[None], (DEVICES, 8, LANES))
    row_copy.wait()


def window(me, leaf_count, received, leaves, up):
    return pl.pallas_call(
        window_kernel,
        in_specs=[smem, smem, vmem, vmem, vmem],
        out_specs=[vmem, smem, smem],
        out_shape=[
            jax.ShapeDtypeStruct((DEVICES, 8, LANES), jnp.float32),
            jax.ShapeDtypeStruct((1, DEVICES), jnp.int32),
            jax.ShapeDtypeStruct((1,), jnp.int32),
        ],
        scratch_shapes=[
            pltpu.VMEM((PAD, LEAVES + LANES), jnp.float32),
            pltpu.VMEM((NC, PAD, LANES), jnp.float32),
            pltpu.VMEM((PAD, LANES), jnp.float32),
            pltpu.VMEM((8, DEVICES), jnp.int32),
            pltpu.SemaphoreType.DMA,
        ],
        compiler_params=pltpu.CompilerParams(vmem_limit_bytes=12 * MiB),
        cost_estimate=pl.CostEstimate(flops=10**7, bytes_accessed=3 * 10**6, transcendentals=0),
        name="window",
    )(me, leaf_count, received, leaves, up)


def top_kernel(
    firsts, lists, windows, raw, out, tables, table, picked, turned, square, rows
):
    tables[...] = jnp.zeros_like(tables)
    picked[...] = jnp.zeros_like(picked)
    rows[...] = jnp.zeros_like(rows)
    square[...] = jnp.zeros_like(square)
    lane = lane_ids()
    first_row = lax.broadcasted_iota(jnp.int32, (8, LANES), 0) == 0

    def put(sender, third):
        at = firsts[0, sender]
        x = windows[sender]
        last = pltpu.roll(x, LANES - PAD, 1)
        tables[third, pl.ds(at, 8), :] = jnp.where(lane < PAD, x, 0.0)
        tables[third, pl.ds(at + 8, 8), :] = jnp.where(first_row & (lane < PAD), last, 0.0)

    @pl.loop(0, DEVICES // 3, unroll=2)
    def _(group):
        for third in range(3):
            put(group * 3 + third, third)

    for sender in range(DEVICES // 3 * 3, DEVICES):
        put(sender, sender % 3)
    table[...] = tables[0] + tables[1] + tables[2]

    for b in range(WIN):
        for c in range(0, CLASSES, 8):
            picks = [lists[b, c + s] for s in range(min(8, CLASSES - c))]
            picked[b % 2, c : c + len(picks), :] = gather_rows(table, picks)[: len(picks)]
        for block in range(0, 2 * LANES, LANES):
            turned[b, :, block : block + LANES] = picked[b % 2, block : block + LANES, :].T[0:PAD, :]
    square[:, 0:NC, 0:CLASSES] = raw[...]

    @pl.loop(0, NC, unroll=5)
    def _(i):
        for b in range(WIN):
            product = None
            for g in range(0, PAD, 8):
                for block in range(0, 2 * LANES, LANES):
                    cols = slice(block, block + LANES)
                    term = square[i, g : g + 8, cols] * turned[b, g : g + 8, cols]
                    product = term if product is None else product + term
            rows[b, pl.ds(i, 1), :] = jnp.sum(product, axis=0, keepdims=True)

    lane = lane_ids(PAD)
    columns = jnp.zeros((PAD, LANES), jnp.float32)
    for b in range(WIN):
        columns = jnp.where(lane == b, jnp.sum(rows[b], axis=1, keepdims=True), columns)
    out[...] = columns


def top(firsts, lists, windows, operators):
    return pl.pallas_call(
        top_kernel,
        in_specs=[smem, smem, vmem, vmem],
        out_specs=vmem,
        out_shape=jax.ShapeDtypeStruct((PAD, LANES), jnp.float32),
        scratch_shapes=[
            pltpu.VMEM((3, TOP_ROWS, LANES), jnp.float32),
            pltpu.VMEM((TOP_ROWS, LANES), jnp.float32),
            pltpu.VMEM((2, 2 * LANES, LANES), jnp.float32),
            pltpu.VMEM((WIN, PAD, 2 * LANES), jnp.float32),
            pltpu.VMEM((NC, PAD, 2 * LANES), jnp.float32),
            pltpu.VMEM((WIN, PAD, LANES), jnp.float32),
        ],
        compiler_params=pltpu.CompilerParams(vmem_limit_bytes=12 * MiB),
        cost_estimate=pl.CostEstimate(flops=10**8, bytes_accessed=20 * 10**6, transcendentals=0),
        name="top",
    )(firsts, lists, windows, operators)


def exchange(x):
    return lax.all_to_all(x, axes, split_axis=0, concat_axis=0, tiled=True)


def per_device(
    leaf_multipoles,
    leaf_count,
    send_boxes,
    leaf_sources,
    top_sources,
    m2l_leaf,
    m2l_top,
    m2m_up,
    l2l_down,
):
    packed = pack(leaf_count, send_boxes[0], leaf_multipoles)
    received = exchange(packed.reshape(DEVICES, 1, -1)).reshape(packed.shape)

    operators = pieces(m2l_leaf)
    lists = leaf_sources.reshape(STEPS, STEP * LEAVES // LANES, LANES)
    top_lists = jnp.transpose(top_sources[0])
    received, operators, lists, top_lists = lax.optimization_barrier(
        (received, operators, lists, top_lists)
    )

    me = lax.axis_index(axes).astype(jnp.int32).reshape(1)
    up = jnp.transpose(m2m_up, (1, 2, 0))
    sent, firsts, shift = window(me, leaf_count, received, leaf_multipoles, up)
    windows = exchange(sent)

    far_field = far(lists, received, leaf_multipoles, operators)
    windows, far_field = lax.optimization_barrier((windows, far_field))
    top_local = top(firsts, top_lists, windows, jnp.transpose(m2l_top, (1, 2, 0)))
    live_mask = jnp.arange(LEAVES) < leaf_count[0]
    spread = jnp.einsum(
        "qik,kb->ibq", l2l_down, top_local[:NC, :WIN], precision=highest
    ).reshape(NC, WIN * 64)
    inherited = lax.dynamic_slice_in_dim(spread, shift[0], LEAVES, 1)
    return jnp.where(live_mask[None, :], far_field[:NC] + inherited, jnp.float32(0.0))


def solution(mesh):
    in_specs = (
        P(None, axes),
        P(axes),
        P(axes, None, None),
        P(axes, None, None),
        P(axes, None, None),
        P(),
        P(),
        P(),
        P(),
    )
    return jax.shard_map(
        per_device, mesh=mesh, in_specs=in_specs, out_specs=P(None, axes), check_vma=False
    )
```

```python
import jax
import jax.numpy as jnp
from jax import lax
from jax.experimental import pallas as pl
from jax.experimental.pallas import tpu as pltpu
from jax.sharding import PartitionSpec as P

NC = 35
CLASSES = 189
LEAVES = 512
SCAP = 64
DEVICES = 128
WIN = 9
PAD = 40
HIGH = 48
LANES = 128
STEP = 7
STEPS = CLASSES // STEP
ROWS = LEAVES + DEVICES * SCAP + 8
TOP_ROWS = 1040
TOP_STEP = 9
PEERS = 16
SENDERS = 16
SENT = 19
THREE = 3 * NC
MiB = 2**20

highest = lax.Precision.HIGHEST
axes = ("gx", "gy")
smem = pl.BlockSpec(memory_space=pltpu.SMEM)
vmem = pl.BlockSpec(memory_space=pltpu.VMEM)
anywhere = pl.BlockSpec(memory_space=pl.ANY)


def lane_ids(rows=8):
    return lax.broadcasted_iota(jnp.int32, (rows, LANES), 1)


def split(x):
    high = x.astype(jnp.bfloat16).astype(jnp.float32)
    return high, x - high


def gather_rows(table, picks):
    sub = lax.broadcasted_iota(jnp.int32, (8, LANES), 0)
    block = None
    for s, pick in enumerate(picks):
        row = jnp.broadcast_to(table[pl.ds(pick, 1), :], (8, LANES))
        block = row if block is None else jnp.where(sub == s, row, block)
    return block


def dot_nt(a, b):
    return lax.dot_general(a, b, (((1,), (1,)), ((), ())), preferred_element_type=jnp.float32)


def operator_pieces(padded, operator):
    padded[0:NC, 0:NC] = operator
    high, low = split(padded[...])
    both = high + pltpu.roll(high, PAD, 1) + pltpu.roll(low, 2 * PAD, 1)
    return both.astype(jnp.bfloat16)


def pack_kernel(count, boxes, leaves, out, stack, table, tail, first, second, sem):
    slots = (first, second)

    def fetch(step, slot):
        rows = pl.ds(step * PEERS, PEERS)
        return pltpu.make_async_copy(boxes.at[rows], slots[slot], sem.at[slot])

    fetch(0, 0).start()
    fetch(1, 1).start()
    for start in range(0, THREE, NC):
        stack[start : start + NC, :] = leaves[...]
    stack[THREE:LANES, :] = leaves[0 : LANES - THREE, :]
    for block in range(0, LEAVES, LANES):
        table[block : block + LANES, :] = stack[:, block : block + LANES].T
    stack[...] = jnp.zeros_like(stack)
    stack[THREE : THREE + NC - 23, :] = leaves[23:NC, :]
    stack[LANES - 8 : LANES, :] = jnp.full((8, LEAVES), count[0].astype(jnp.float32))
    for block in range(0, LEAVES, LANES):
        tail[block : block + LANES, :] = stack[:, block : block + LANES].T
    lane = lane_ids()

    def work(step, slot):
        fetch(step, slot).wait()
        for peer in range(PEERS):
            for r in range(0, SENT, 8):
                size = min(8, SENT - r)
                a, b, c = (
                    gather_rows(table, [slots[slot][peer, g * SENT + r + s] for s in range(size)])
                    for g in range(3)
                )
                block = jnp.where(lane < NC, a, jnp.where(lane < 2 * NC, b, c))
                ends = []
                for row in range(r, min(r + 8, 14)):
                    pick = slots[slot][peer, 3 * SENT + row % 7]
                    ends.append((table if row < 7 else tail)[pl.ds(pick, 1), :])
                if ends:
                    sub = lax.broadcasted_iota(jnp.int32, (8, LANES), 0)
                    end = jnp.broadcast_to(ends[0], (8, LANES))
                    for s in range(1, len(ends)):
                        end = jnp.where(sub == s, jnp.broadcast_to(ends[s], (8, LANES)), end)
                    block = jnp.where(lane < THREE, block, end)
                at = step * (PEERS * SENT) + peer * SENT + r
                out[pl.ds(at, size), :] = block[:size]

        @pl.when(step + 2 < DEVICES // PEERS)
        def _():
            fetch(step + 2, slot).start()

    @pl.loop(0, DEVICES // PEERS // 2)
    def _(pair):
        work(2 * pair, 0)
        work(2 * pair + 1, 1)


def pack(leaf_count, boxes, leaves):
    return pl.pallas_call(
        pack_kernel,
        in_specs=[smem, anywhere, vmem],
        out_specs=vmem,
        out_shape=jax.ShapeDtypeStruct((DEVICES * SENT, LANES), jnp.float32),
        scratch_shapes=[
            pltpu.VMEM((LANES, LEAVES), jnp.float32),
            pltpu.VMEM((LEAVES, LANES), jnp.float32),
            pltpu.VMEM((LEAVES, LANES), jnp.float32),
            pltpu.SMEM((PEERS, SCAP), jnp.int32),
            pltpu.SMEM((PEERS, SCAP), jnp.int32),
            pltpu.SemaphoreType.DMA((2,)),
        ],
        compiler_params=pltpu.CompilerParams(vmem_limit_bytes=8 * MiB),
        cost_estimate=pl.CostEstimate(flops=10**6, bytes_accessed=18 * 10**6, transcendentals=0),
        name="pack",
    )(leaf_count, boxes, leaves)


def pieces_kernel(raw, operators, square):
    square[...] = jnp.zeros_like(square)

    @pl.loop(0, STEPS)
    def _(step):
        for c in range(STEP):
            cols = slice(c * LANES, (c + 1) * LANES)
            operators[step, :, cols] = operator_pieces(square, raw[step * STEP + c])


def pieces(raw):
    return pl.pallas_call(
        pieces_kernel,
        in_specs=[vmem],
        out_specs=vmem,
        out_shape=jax.ShapeDtypeStruct((STEPS, HIGH, STEP * LANES), jnp.bfloat16),
        scratch_shapes=[pltpu.VMEM((HIGH, LANES), jnp.float32)],
        compiler_params=pltpu.CompilerParams(vmem_limit_bytes=12 * MiB),
        cost_estimate=pl.CostEstimate(flops=10**6, bytes_accessed=8 * 10**6, transcendentals=0),
        name="pieces",
    )(raw)


def far_kernel(
    lists, received, leaves, operators, out, padded, table, spread, made, even, odd, one, two, sem
):
    slots, picked = (one, two), (even, odd)

    def fetch(step, slot):
        return pltpu.make_async_copy(lists.at[step], slots[slot], sem.at[slot])

    fetch(0, 0).start()
    fetch(1, 1).start()
    out[...] = jnp.zeros_like(out)
    odd[...] = jnp.zeros_like(odd)
    padded[...] = jnp.zeros_like(padded)
    padded[0:NC, :] = leaves[...]
    rest = jnp.zeros((LANES - 3 * PAD, LANES), jnp.float32)
    for block in range(0, LEAVES, LANES):
        high, low = split(padded[:, block : block + LANES])
        table[block : block + LANES, :] = jnp.concatenate([high, low, high, rest], axis=0).T
    table[ROWS - 8 : ROWS, :] = jnp.zeros((8, LANES), jnp.float32)

    source = lax.broadcasted_iota(jnp.int32, (2 * LANES, 5 * LANES), 0)
    place = lax.broadcasted_iota(jnp.int32, (2 * LANES, 5 * LANES), 1)
    group, at = place >> 7, place & (LANES - 1)
    third = jnp.where(at < PAD, 0, jnp.where(at < 2 * PAD, 1, 2))
    k = at - third * PAD
    wanted = jnp.where(group < 3, group * NC + k, jnp.where(group == 3, THREE + k, THREE - 23 + k))
    wanted = wanted + jnp.where(third == 1, LANES, 0)
    held = (k < NC) & ((group < 3) | ((group == 3) & (k < 23)) | ((group == 4) & (k >= 23)))
    hit = (source == wanted) & held & (at < 3 * PAD)
    spread[...] = jnp.where(hit, 1.0, 0.0).astype(jnp.bfloat16)

    @pl.loop(0, DEVICES // SENDERS)
    def _(step):
        rows = SENDERS * SENT
        x = received[pl.ds(pl.multiple_of(step * rows, 8), rows), :]
        both = jnp.concatenate(split(x), axis=1).astype(jnp.bfloat16)
        made[...] = jnp.dot(both, spread[...], preferred_element_type=jnp.float32)
        for sender in range(SENDERS):
            base = LEAVES + (step * SENDERS + sender) * SCAP
            top_row = sender * SENT
            for g in range(3):
                for r in range(0, SENT, 8):
                    size = min(8, SENT - r)
                    block = made[top_row + r : top_row + r + size, g * LANES : (g + 1) * LANES]
                    table[pl.ds(base + g * SENT + r, size), :] = block
            ends = made[top_row : top_row + 7, 3 * LANES : 4 * LANES]
            ends += made[top_row + 7 : top_row + 14, 4 * LANES : 5 * LANES]
            table[pl.ds(base + 3 * SENT, 7), :] = ends

    def multiply(step, slot):
        out[...] += dot_nt(operators[step], picked[slot][...])

    def work(step, slot):
        fetch(step, slot).wait()
        for row in range(0, STEP * LEAVES, 16):
            places = [row + s for s in range(16)]
            picks = [slots[slot][p // LANES, p % LANES] for p in places]
            block = [gather_rows(table, picks[0:8]), gather_rows(table, picks[8:16])]
            c, t = row // LEAVES, row % LEAVES
            block = jnp.concatenate(block, axis=0).astype(jnp.bfloat16)
            picked[slot][t : t + 16, c * LANES : (c + 1) * LANES] = block
        multiply(jnp.maximum(step - 1, 0), 1 - slot)

        @pl.when(step + 2 < STEPS)
        def _():
            fetch(step + 2, slot).start()


    @pl.loop(0, STEPS // 2)
    def _(pair):
        work(2 * pair, 0)
        work(2 * pair + 1, 1)

    work(STEPS - 1, 0)
    multiply(STEPS - 1, 0)


def far(lists, received, leaves, operators):
    return pl.pallas_call(
        far_kernel,
        in_specs=[anywhere] + [vmem] * 3,
        out_specs=vmem,
        out_shape=jax.ShapeDtypeStruct((HIGH, LEAVES), jnp.float32),
        scratch_shapes=[
            pltpu.VMEM((PAD, LEAVES), jnp.float32),
            pltpu.VMEM((ROWS, LANES), jnp.float32),
            pltpu.VMEM((2 * LANES, 5 * LANES), jnp.bfloat16),
            pltpu.VMEM((SENDERS * SENT, 5 * LANES), jnp.float32),
            pltpu.VMEM((LEAVES, STEP * LANES), jnp.bfloat16),
            pltpu.VMEM((LEAVES, STEP * LANES), jnp.bfloat16),
            pltpu.SMEM((STEP * LEAVES // LANES, LANES), jnp.int32),
            pltpu.SMEM((STEP * LEAVES // LANES, LANES), jnp.int32),
            pltpu.SemaphoreType.DMA((2,)),
        ],
        compiler_params=pltpu.CompilerParams(vmem_limit_bytes=16 * MiB),
        cost_estimate=pl.CostEstimate(flops=10**9, bytes_accessed=100 * 10**6, transcendentals=0),
        name="far",
    )(lists, received, leaves, operators)


def window_kernel(
    me, count, received, leaves, both, out, starts, shift,
    padded, rows, row, row_sem,
):
    live = lax.broadcasted_iota(jnp.int32, (NC, LEAVES), 1) < count[0]
    padded[...] = jnp.zeros_like(padded)
    padded[0:NC, 0:LEAVES] = jnp.where(live, leaves[...], 0.0)
    rows[...] = jnp.zeros_like(rows)

    lane = lane_ids(DEVICES)
    sender = lax.broadcasted_iota(jnp.int32, (DEVICES, LANES), 0)
    heads = [[(s + r) * SENT + 7 for r in range(8)] for s in range(0, DEVICES, 8)]
    heads = jnp.concatenate([gather_rows(received, picks) for picks in heads], axis=0)
    counts = jnp.where(lane == LANES - 1, heads, 0.0)
    large = jnp.floor(counts * 0.0625)
    small = counts - 16.0 * large
    lower = jnp.where(lane < sender, 1.0, 0.0).astype(jnp.bfloat16)

    def sums(x):
        return jnp.dot(lower, x.astype(jnp.bfloat16), preferred_element_type=jnp.float32)

    before = 16.0 * sums(large) + sums(small)
    row[...] = before.T[LANES - 8 : LANES, :].astype(jnp.int32) >> 6
    row_copy = pltpu.make_async_copy(row.at[pl.ds(7, 1), :], starts, row_sem)
    row_copy.start()
    first_leaf = jnp.sum(jnp.where(sender == me[0], before, 0.0)).astype(jnp.int32)
    shift_in = first_leaf & 63
    shift[0] = shift_in
    placed = pltpu.roll(padded[...], shift_in, 1)

    lane = lane_ids(PAD)
    columns = jnp.zeros((PAD, LANES), jnp.float32)
    for t in range(5):
        cols = slice(t * LANES, (t + 1) * LANES)
        for i in range(NC):
            product = both[i, 0:8, :] * placed[0:8, cols]
            for g in range(8, PAD, 8):
                product += both[i, g : g + 8, :] * placed[g : g + 8, cols]
            rows[i : i + 1, :] = jnp.sum(product, axis=0, keepdims=True)
        for half in range(2):
            mine = (lane < 64) if half == 0 else (lane >= 64)
            column = jnp.sum(jnp.where(mine, rows[...], 0.0), axis=1, keepdims=True)
            columns = jnp.where(lane == 2 * t + half, column, columns)
    rest = jnp.zeros((LANES - PAD, LANES), jnp.float32)
    turned = jnp.concatenate([columns, rest], axis=0).T
    last = pltpu.roll(turned[8:16, :], PAD, 1)
    sub = lax.broadcasted_iota(jnp.int32, (8, LANES), 0)
    block = turned[0:8, :] + jnp.where(sub == 0, last, 0.0)
    out[...] = jnp.broadcast_to(block[None], (DEVICES, 8, LANES))
    row_copy.wait()


def window(me, leaf_count, received, leaves, up):
    return pl.pallas_call(
        window_kernel,
        in_specs=[smem, smem, vmem, vmem, vmem],
        out_specs=[vmem, smem, smem],
        out_shape=[
            jax.ShapeDtypeStruct((DEVICES, 8, LANES), jnp.float32),
            jax.ShapeDtypeStruct((1, DEVICES), jnp.int32),
            jax.ShapeDtypeStruct((1,), jnp.int32),
        ],
        scratch_shapes=[
            pltpu.VMEM((PAD, LEAVES + LANES), jnp.float32),
            pltpu.VMEM((PAD, LANES), jnp.float32),
            pltpu.VMEM((8, DEVICES), jnp.int32),
            pltpu.SemaphoreType.DMA,
        ],
        compiler_params=pltpu.CompilerParams(vmem_limit_bytes=12 * MiB),
        cost_estimate=pl.CostEstimate(flops=10**7, bytes_accessed=3 * 10**6, transcendentals=0),
        name="window",
    )(me, leaf_count, received, leaves, up)


def top_kernel(
    firsts, lists, windows, square, out, tables, table, picked, turned, rows
):
    tables[...] = jnp.zeros_like(tables)
    picked[...] = jnp.zeros_like(picked)
    rows[...] = jnp.zeros_like(rows)
    lane = lane_ids()
    first_row = lax.broadcasted_iota(jnp.int32, (8, LANES), 0) == 0

    def put(sender, third):
        at = firsts[0, sender]
        x = windows[sender]
        last = pltpu.roll(x, LANES - PAD, 1)
        tables[third, pl.ds(at, 8), :] = jnp.where(lane < PAD, x, 0.0)
        tables[third, pl.ds(at + 8, 8), :] = jnp.where(first_row & (lane < PAD), last, 0.0)

    @pl.loop(0, DEVICES // 3, unroll=2)
    def _(group):
        for third in range(3):
            put(group * 3 + third, third)

    for sender in range(DEVICES // 3 * 3, DEVICES):
        put(sender, sender % 3)
    table[...] = tables[0] + tables[1] + tables[2]

    for b in range(WIN):
        for c in range(0, CLASSES, 8):
            picks = [lists[b, c + s] for s in range(min(8, CLASSES - c))]
            picked[b % 2, c : c + len(picks), :] = gather_rows(table, picks)[: len(picks)]
        for block in range(0, 2 * LANES, LANES):
            turned[b, :, block : block + LANES] = picked[b % 2, block : block + LANES, :].T[0:PAD, :]

    @pl.loop(0, NC, unroll=5)
    def _(i):
        for b in range(WIN):
            product = None
            for g in range(0, PAD, 8):
                for block in range(0, 2 * LANES, LANES):
                    cols = slice(block, block + LANES)
                    term = square[i, g : g + 8, cols] * turned[b, g : g + 8, cols]
                    product = term if product is None else product + term
            rows[b, pl.ds(i, 1), :] = jnp.sum(product, axis=0, keepdims=True)

    lane = lane_ids(PAD)
    columns = jnp.zeros((PAD, LANES), jnp.float32)
    for b in range(WIN):
        columns = jnp.where(lane == b, jnp.sum(rows[b], axis=1, keepdims=True), columns)
    out[...] = columns


def top(firsts, lists, windows, operators):
    return pl.pallas_call(
        top_kernel,
        in_specs=[smem, smem, vmem, vmem],
        out_specs=vmem,
        out_shape=jax.ShapeDtypeStruct((PAD, LANES), jnp.float32),
        scratch_shapes=[
            pltpu.VMEM((3, TOP_ROWS, LANES), jnp.float32),
            pltpu.VMEM((TOP_ROWS, LANES), jnp.float32),
            pltpu.VMEM((2, 2 * LANES, LANES), jnp.float32),
            pltpu.VMEM((WIN, PAD, 2 * LANES), jnp.float32),
            pltpu.VMEM((WIN, PAD, LANES), jnp.float32),
        ],
        compiler_params=pltpu.CompilerParams(vmem_limit_bytes=12 * MiB),
        cost_estimate=pl.CostEstimate(flops=10**8, bytes_accessed=20 * 10**6, transcendentals=0),
        name="top",
    )(firsts, lists, windows, operators)


def exchange(x):
    return lax.all_to_all(x, axes, split_axis=0, concat_axis=0, tiled=True)


def per_device(
    leaf_multipoles,
    leaf_count,
    send_boxes,
    leaf_sources,
    top_sources,
    m2l_leaf,
    m2l_top,
    m2m_up,
    l2l_down,
):
    packed = pack(leaf_count, send_boxes[0], leaf_multipoles)
    received = exchange(packed.reshape(DEVICES, 1, -1)).reshape(packed.shape)

    operators = pieces(m2l_leaf)
    lists = leaf_sources.reshape(STEPS, STEP * LEAVES // LANES, LANES)
    top_lists = jnp.transpose(top_sources[0])
    rows = (0, PAD - NC)
    up = jnp.pad(jnp.transpose(m2m_up, (1, 2, 0)), ((0, 0), rows, (0, 0)))
    up = jnp.concatenate([up, up], axis=2)
    square = jnp.pad(
        jnp.transpose(m2l_top, (1, 2, 0)), ((0, 0), rows, (0, 2 * LANES - CLASSES))
    )
    received, operators, lists, top_lists, up, square = lax.optimization_barrier(
        (received, operators, lists, top_lists, up, square)
    )

    me = lax.axis_index(axes).astype(jnp.int32).reshape(1)
    sent, firsts, shift = window(me, leaf_count, received, leaf_multipoles, up)
    windows = exchange(sent)

    far_field = far(lists, received, leaf_multipoles, operators)
    windows, far_field = lax.optimization_barrier((windows, far_field))
    top_local = top(firsts, top_lists, windows, square)
    live_mask = jnp.arange(LEAVES) < leaf_count[0]
    spread = jnp.einsum(
        "qik,kb->ibq", l2l_down, top_local[:NC, :WIN], precision=highest
    ).reshape(NC, WIN * 64)
    inherited = lax.dynamic_slice_in_dim(spread, shift[0], LEAVES, 1)
    return jnp.where(live_mask[None, :], far_field[:NC] + inherited, jnp.float32(0.0))


def solution(mesh):
    in_specs = (
        P(None, axes),
        P(axes),
        P(axes, None, None),
        P(axes, None, None),
        P(axes, None, None),
        P(),
        P(),
        P(),
        P(),
    )
    return jax.shard_map(
        per_device, mesh=mesh, in_specs=in_specs, out_specs=P(None, axes), check_vma=False
    )
```
